32 devices in a mesh: gx: 4 (over z), yz: 8 (over y, x, core).
Axes of the slice: x: 2, y: 2, z: 4, core: 2. Of those that a mesh axis runs over, the one named last changes fastest.
Arguments:
- features: bfloat16 [384, 96, 512], P(('gx', 'yz')), may hold values from -6 to 6
- occupancy: int32 [384, 512], P(('gx', 'yz')), may hold values 0 or 1
- neighbours: int32 [384, 27], P(('gx', 'yz')), may hold values from 0 to 84, as said below
- exports: int32 [256], P(('gx', 'yz')), may hold values from 0 to 11, as said below
- coarse_map: int32 [384, 2], P(('gx', 'yz')), may hold values from 0 to 7, as said below
- owners: int32 [128], P(('gx', 'yz')), may hold values from 0 to 7, as said below
- w_sub: bfloat16 [27, 96, 96], replicated, may hold values from -0.15625 to 0.15625
- w_down: bfloat16 [8, 192, 96], replicated, may hold values from -0.3125 to 0.3125
- cotangent: bfloat16 [256, 192, 512], P(('gx', 'yz')), may hold values from -6 to 6
Outputs:
- coarse: bfloat16 [256, 192, 512], P(('gx', 'yz'))
- grad_features: bfloat16 [384, 96, 512], P(('gx', 'yz'))
- grad_sub: float32 [27, 96, 96], replicated
- grad_down: float32 [8, 192, 96], replicated
The draws below stay inside these ranges and needn't reach their ends.
Inputs may be any that keep to these rules, and one draw needn't show every extreme that they name: `neighbours`: entry 13 of a brick is its own slot. Entries follow the geometry of a map of 8-voxel bricks in which device (i, j) holds a region of 4 x 4 x 2 brick cells beside the regions of (i +- 1, j +- 1); a brick met at offset k meets the first at the opposite offset. Entries that point to another device name only bricks on that device's side faces. `exports`: each device's 8 entries are distinct slots of its bricks that lie on its region's side faces, and every such brick is listed. `coarse_map`: column 0 is the coarse cell (0 to 3), column 1 the octant; every coarse cell of every device holds exactly 3 of its fine bricks, in distinct octants. The 4 coarse cells of one device have distinct owners; in every gx slab one owner is named by every device of the slab.
All inputs are finite; a program needn't handle non-finite values. No bound on the sum of `occupancy` on one device may be relied on, other than what follows from the above.
Results may differ from the reference program's by a relative error of at most 0.0062.
Values may be sent and summed in bfloat16 or wider, within the bound.
A program may use at most 320 MiB of HBM per device.

```python
import jax
import jax.numpy as jnp
from jax import lax

C1 = 96
C2 = 192
EDGE = 8
RZ = 2
VOX = 512
HALF = 4
CVOX = 64
QC = 4
BR = 12
EXP = 8
NF = 384
NCO = 256
N_GX = 4
N_YZ = 8


def layout(key):
    base = jax.random.fold_in(key, 11)
    keys = jax.random.split(base, 6)
    devices = N_GX * N_YZ
    cell_ids = jnp.arange(QC, dtype=jnp.int32)
    cell_z = cell_ids // 4
    cell_x = cell_ids // 2 % 2
    cell_y = cell_ids % 2
    octants = jnp.arange(8, dtype=jnp.int32)
    octant_x = octants // 4
    octant_y = octants // 2 % 2
    octant_z = octants % 2
    inner = (octant_x[None, :] == 1 - cell_x[:, None]) & (octant_y[None, :] == 1 - cell_y[:, None])
    scores = jax.random.randint(keys[0], (devices, QC, 8), 0, 1 << 20) * 8 + octants
    outer_order = jnp.argsort(-jnp.where(inner[None], -1, scores), axis=-1)[..., :2]
    inner_order = jnp.argsort(-jnp.where(inner[None], scores, -1), axis=-1)[..., :1]
    chosen = jnp.concatenate([outer_order, inner_order], axis=-1).astype(jnp.int32)
    brick_oct = chosen.reshape(devices, BR)
    brick_cell = jnp.repeat(cell_ids, 3)
    brick_side = jnp.tile(jnp.array([1, 1, 0], jnp.int32), QC)
    slot_scores = jax.random.randint(keys[1], (devices, BR), 0, 1 << 20) * BR + jnp.arange(BR, dtype=jnp.int32)
    slot_of = jnp.argsort(slot_scores, axis=-1).astype(jnp.int32)
    member = jnp.argsort(slot_of, axis=-1).astype(jnp.int32)
    map_cell = jnp.take(brick_cell, member)
    map_oct = jnp.take_along_axis(brick_oct, member, axis=1)
    coarse_map = jnp.stack([map_cell, map_oct], axis=-1).reshape(devices * BR, 2)
    export_scores = jax.random.randint(keys[2], (devices, BR), 0, 1 << 20) * BR + jnp.arange(BR, dtype=jnp.int32)
    export_order = jnp.argsort(-jnp.where(brick_side[None, :] == 1, export_scores, -1), axis=-1)[:, :EXP]
    export_slots = jnp.take_along_axis(slot_of, export_order, axis=1).astype(jnp.int32)
    device_ids = jnp.arange(devices, dtype=jnp.int32)
    export_gid = (device_ids[:, None] * BR + export_slots).reshape(-1)
    export_pos = jnp.zeros((devices * BR,), jnp.int32).at[export_gid].set(jnp.tile(jnp.arange(EXP, dtype=jnp.int32), devices))
    row_of = device_ids // N_YZ
    col_of = device_ids % N_YZ
    fine_x = (4 * row_of[:, None] + 2 * cell_x[map_cell] + octant_x[map_oct]).reshape(-1)
    fine_y = (4 * col_of[:, None] + 2 * cell_y[map_cell] + octant_y[map_oct]).reshape(-1)
    fine_z = (2 * cell_z[map_cell] + octant_z[map_oct]).reshape(-1)
    gids = jnp.arange(devices * BR, dtype=jnp.int32)
    occupied = jnp.full((4 * N_GX, 4 * N_YZ, RZ), -1, jnp.int32).at[fine_x, fine_y, fine_z].set(gids)
    offsets = jnp.arange(27, dtype=jnp.int32)
    near_x = fine_x[:, None] + offsets // 9 - 1
    near_y = fine_y[:, None] + offsets // 3 % 3 - 1
    near_z = fine_z[:, None] + offsets % 3 - 1
    inside = (near_x >= 0) & (near_x < 4 * N_GX) & (near_y >= 0) & (near_y < 4 * N_YZ) & (near_z >= 0) & (near_z < RZ)
    found = occupied[jnp.clip(near_x, 0, 4 * N_GX - 1), jnp.clip(near_y, 0, 4 * N_YZ - 1), jnp.clip(near_z, 0, RZ - 1)]
    valid = inside & (found >= 0)
    safe = jnp.maximum(found, 0)
    near_dev = safe // BR
    home_dev = gids // BR
    same = near_dev == home_dev[:, None]
    across = BR + ((near_dev // N_YZ - (home_dev // N_YZ)[:, None] + 1) * 3 + (near_dev % N_YZ - (home_dev % N_YZ)[:, None] + 1)) * EXP + jnp.take(export_pos, safe)
    entry = jnp.where(same, safe % BR, across)
    neighbours = jnp.where(valid, entry, BR + 9 * EXP).astype(jnp.int32)
    star = jax.random.randint(keys[3], (N_GX,), 0, N_YZ)
    star_dev = jnp.take(star, row_of)
    other_scores = jax.random.randint(keys[4], (devices, N_YZ - 1), 0, 1 << 20) * (N_YZ - 1) + jnp.arange(N_YZ - 1, dtype=jnp.int32)
    others = jnp.argsort(other_scores, axis=-1)[:, :QC - 1].astype(jnp.int32)
    others = others + (others >= star_dev[:, None]).astype(jnp.int32)
    combined = jnp.concatenate([star_dev[:, None], others], axis=1)
    shuffle = jnp.argsort(jax.random.randint(keys[5], (devices, QC), 0, 1 << 20) * QC + jnp.arange(QC, dtype=jnp.int32), axis=-1)
    owners = jnp.take_along_axis(combined, shuffle, axis=1).reshape(-1).astype(jnp.int32)
    return (neighbours, export_slots.reshape(-1), coarse_map.astype(jnp.int32), owners)


def draw_neighbours(key, part):
    return layout(key)[0]


def draw_exports(key, part):
    return layout(key)[1]


def draw_coarse_map(key, part):
    return layout(key)[2]


def draw_owners(key, part):
    return layout(key)[3]


def touch_ends(entries, own_key, least, top_value):
    spot = [jax.random.randint(jax.random.fold_in(own_key, axis), (), 0, length) for axis, length in enumerate(entries.shape)]
    main_axis = entries.shape.index(max(entries.shape))
    next_to = spot[:main_axis] + [(spot[main_axis] + 1) % entries.shape[main_axis]] + spot[main_axis + 1:]
    return entries.at[tuple(spot)].set(least).at[tuple(next_to)].set(top_value)


def block_scale(rng, dims, shards, low, top_value):
    def one(axis_at, parts):
        draws = jax.random.uniform(jax.random.fold_in(jax.random.fold_in(rng, 6), axis_at), (parts,), jnp.float32, low / len(shards), top_value / len(shards))
        return jnp.repeat(jnp.exp(draws), dims[axis_at] // parts).reshape((-1,) + (1,) * (len(dims) - axis_at - 1))

    factor_of = one(*shards[0])
    for cut in shards[1:]:
        factor_of = factor_of * one(*cut)
    return factor_of


def centred(key, shape, spread, most, cuts=(), held_as=jnp.bfloat16):
    loudness = block_scale(key, shape, cuts, -0.22, 0.18) if cuts else 1.0
    values = jax.random.normal(key, shape, jnp.float32) * spread * loudness
    return jnp.minimum(jnp.maximum(values, -most), most).astype(held_as)


def setup_inputs(seed: int = 0) -> dict:
    streams_of = jax.random.split(jax.random.key(seed), 10)
    features = centred(streams_of[0], (NF, C1, VOX), 1.0, 6.0, ((0, 32),))
    occupancy = touch_ends((jax.random.randint(streams_of[1], (NF, VOX), 0, 2) < 1).astype(jnp.int32), jax.random.fold_in(streams_of[1], 1), 0, 1)
    neighbours = draw_neighbours(jax.random.fold_in(streams_of[9], 71), 0)
    exports = draw_exports(jax.random.fold_in(streams_of[9], 71), 0)
    coarse_map = draw_coarse_map(jax.random.fold_in(streams_of[9], 71), 0)
    owners = draw_owners(jax.random.fold_in(streams_of[9], 71), 0)
    w_sub = centred(streams_of[6], (27, C1, C1), (13 * C1) ** -0.5, 0.15625)
    w_down = centred(streams_of[7], (8, C2, C1), (4 * C1) ** -0.5, 0.3125)
    cotangent = centred(streams_of[8], (NCO, C2, VOX), 1.0, 6.0, ((0, 32),))
    return dict(features=features, occupancy=occupancy, neighbours=neighbours, exports=exports, coarse_map=coarse_map, owners=owners, w_sub=w_sub, w_down=w_down, cotangent=cotangent)


def silu_slope(values):
    sig = jax.nn.sigmoid(values)
    return sig * (1.0 + values * (1.0 - sig))


def layer_span(shift, cube_edge):
    if shift < 0:
        return slice(cube_edge - 1, cube_edge), slice(0, 1)
    if shift > 0:
        return slice(0, 1), slice(cube_edge + 1, cube_edge + 2)
    return slice(0, cube_edge), slice(1, cube_edge + 1)


def pad_bricks(lookup, neighbour_ids, cube_edge):
    channels = lookup.shape[1]
    blocks = lookup.reshape(lookup.shape[0], channels, cube_edge, cube_edge, cube_edge)
    padded = jnp.zeros((neighbour_ids.shape[0], channels, cube_edge + 2, cube_edge + 2, cube_edge + 2), lookup.dtype)
    for offset in range(27):
        spans = [layer_span(shift, cube_edge) for shift in (offset // 9 - 1, offset // 3 % 3 - 1, offset % 3 - 1)]
        facing = blocks[:, :, spans[0][0], spans[1][0], spans[2][0]]
        picked = jnp.take(facing, neighbour_ids[:, offset], axis=0)
        padded = padded.at[:, :, spans[0][1], spans[1][1], spans[2][1]].set(picked)
    return padded


def conv_forward(padded, weights, cube_edge):
    result = None
    for offset in range(27):
        start_x, start_y, start_z = offset // 9, offset // 3 % 3, offset % 3
        window = padded[:, :, start_x:start_x + cube_edge, start_y:start_y + cube_edge, start_z:start_z + cube_edge]
        term = jnp.einsum("oi,bixyz->boxyz", weights[offset].astype(jnp.float32), window.astype(jnp.float32))
        result = term if result is None else result + term
    return result


def conv_transpose(padded, weights, cube_edge):
    result = None
    for offset in range(27):
        start_x, start_y, start_z = 2 - offset // 9, 2 - offset // 3 % 3, 2 - offset % 3
        window = padded[:, :, start_x:start_x + cube_edge, start_y:start_y + cube_edge, start_z:start_z + cube_edge]
        term = jnp.einsum("oi,boxyz->bixyz", weights[offset].astype(jnp.float32), window.astype(jnp.float32))
        result = term if result is None else result + term
    return result


def conv_weights(padded, grads, cube_edge):
    terms = []
    for offset in range(27):
        start_x, start_y, start_z = offset // 9, offset // 3 % 3, offset % 3
        window = padded[:, :, start_x:start_x + cube_edge, start_y:start_y + cube_edge, start_z:start_z + cube_edge]
        terms.append(jnp.einsum("boxyz,bixyz->oi", grads.astype(jnp.float32), window.astype(jnp.float32)))
    return jnp.stack(terms)


def split_fine(values, half_edge):
    rows, channels = values.shape[0], values.shape[1]
    shaped = values.reshape(rows, channels, half_edge, 2, half_edge, 2, half_edge, 2)
    return shaped.transpose(0, 1, 3, 5, 7, 2, 4, 6).reshape(rows, channels, 8, half_edge ** 3)


def join_fine(values, half_edge):
    rows, channels = values.shape[0], values.shape[1]
    shaped = values.reshape(rows, channels, 2, 2, 2, half_edge, half_edge, half_edge)
    return shaped.transpose(0, 1, 5, 2, 6, 3, 7, 4).reshape(rows, channels, 8 * half_edge ** 3)


def split_block(values, half_edge):
    rows, channels = values.shape[0], values.shape[1]
    shaped = values.reshape(rows, channels, 2, half_edge, 2, half_edge, 2, half_edge)
    return shaped.transpose(0, 1, 2, 4, 6, 3, 5, 7).reshape(rows, channels, 8, half_edge ** 3)


def join_block(values, half_edge):
    rows, channels = values.shape[0], values.shape[1]
    shaped = values.reshape(rows, channels, 2, 2, 2, half_edge, half_edge, half_edge)
    return shaped.transpose(0, 1, 2, 5, 3, 6, 4, 7).reshape(rows, channels, 8 * half_edge ** 3)


def reference(features, occupancy, neighbours, exports, coarse_map, owners, w_sub, w_down, cotangent):
    devices = N_GX * N_YZ
    fine_total = features.shape[0]
    brick_ids = jnp.arange(fine_total, dtype=jnp.int32)
    home = brick_ids // BR
    home_row = home // N_YZ
    home_col = home % N_YZ
    absent = BR + 9 * EXP
    remote = neighbours - BR
    place = remote // EXP
    within = remote % EXP
    peer_row = jnp.clip(home_row[:, None] + place // 3 - 1, 0, N_GX - 1)
    peer_col = jnp.clip(home_col[:, None] + place % 3 - 1, 0, N_YZ - 1)
    peer = peer_row * N_YZ + peer_col
    peer_slot = jnp.take(exports, jnp.clip(peer * EXP + within, 0, devices * EXP - 1))
    global_ids = jnp.where(neighbours < BR, home[:, None] * BR + neighbours,
                           jnp.where(neighbours < absent, peer * BR + peer_slot, fine_total)).astype(jnp.int32)
    id_blocks = global_ids.reshape(devices, BR, 27)

    masked = features * occupancy.astype(jnp.bfloat16)[:, None, :]
    lookup = jnp.concatenate([masked, jnp.zeros((1, C1, VOX), jnp.bfloat16)], axis=0)
    live = occupancy.astype(jnp.float32).reshape(fine_total, 1, EDGE, EDGE, EDGE)

    def forward_block(id_block):
        return conv_forward(pad_bricks(lookup, id_block, EDGE), w_sub, EDGE)

    pre_sub = lax.map(forward_block, id_blocks).reshape(fine_total, C1, EDGE, EDGE, EDGE) * live
    hidden = jax.nn.silu(pre_sub).astype(jnp.bfloat16)
    strided = split_fine(hidden.reshape(fine_total, C1, VOX), HALF)
    piece = jnp.einsum("toi,bitu->bou", w_down.astype(jnp.float32), strided.astype(jnp.float32)).astype(jnp.bfloat16)

    cell_of = coarse_map[:, 0]
    octant_of = coarse_map[:, 1]
    owner_of = jnp.take(owners, home * QC + cell_of)
    row_of = ((home_row * N_YZ + owner_of) * N_YZ + home_col).astype(jnp.int32)
    coarse_oct = jnp.zeros((NCO, C2, 8, CVOX), jnp.bfloat16).at[row_of, :, octant_of].set(piece)
    coarse_pre = join_block(coarse_oct, HALF).astype(jnp.float32)
    coarse = jax.nn.silu(coarse_pre).astype(jnp.bfloat16)
    grad_coarse = (cotangent.astype(jnp.float32) * silu_slope(coarse_pre)).astype(jnp.bfloat16)
    grad_piece = split_block(grad_coarse, HALF)[row_of, :, octant_of]

    grad_down = jnp.einsum("bou,bitu->toi", grad_piece.astype(jnp.float32), strided.astype(jnp.float32))
    grad_hidden = join_fine(jnp.einsum("toi,bou->bitu", w_down.astype(jnp.float32), grad_piece.astype(jnp.float32)), HALF)
    grad_hidden = grad_hidden.reshape(fine_total, C1, EDGE, EDGE, EDGE)
    grad_pre = (grad_hidden * silu_slope(pre_sub) * live).astype(jnp.bfloat16)
    grad_lookup = jnp.concatenate([grad_pre.reshape(fine_total, C1, VOX), jnp.zeros((1, C1, VOX), jnp.bfloat16)], axis=0)

    def backward_block(pair):
        id_block, grad_block = pair
        padded_grad = pad_bricks(grad_lookup, id_block, EDGE)
        padded_input = pad_bricks(lookup, id_block, EDGE)
        return conv_transpose(padded_grad, w_sub, EDGE), conv_weights(padded_input, grad_block, EDGE)

    grad_blocks, sub_terms = lax.map(backward_block, (id_blocks, grad_pre.reshape(devices, BR, C1, EDGE, EDGE, EDGE)))
    grad_sub = jnp.sum(sub_terms, axis=0)
    grad_features = (grad_blocks.reshape(fine_total, C1, EDGE, EDGE, EDGE) * live).reshape(fine_total, C1, VOX).astype(jnp.bfloat16)
    return coarse, grad_features, grad_sub, grad_down
```

```python
import jax
import jax.numpy as jnp
import numpy as np
from jax import lax
from jax.experimental import pallas as pl
from jax.experimental.pallas import tpu as pltpu
from jax.sharding import PartitionSpec as P

EDGE = 8
VOX = 512
LANES = 128
TAPS = 27
VMEM_BYTES = 56 * 2**20


def silu_slope(values):
    sig = jax.nn.sigmoid(values)
    return sig * (1.0 + values * (1.0 - sig))


def fine_order():
    ids = np.arange(VOX).reshape(4, 2, 4, 2, 4, 2).transpose(1, 3, 5, 0, 2, 4).reshape(-1)
    return np.eye(VOX, dtype=np.float32)[ids]


def block_order():
    ids = np.arange(VOX).reshape(2, 4, 2, 4, 2, 4).transpose(0, 2, 4, 1, 3, 5).reshape(-1)
    return np.eye(VOX, dtype=np.float32)[ids].reshape(8, 64, VOX)


def fill_columns(ids, look, pad, col, brick, flip):
    span = {-1: (slice(7, 8), slice(0, 1)), 0: (slice(0, 8), slice(1, 9)), 1: (slice(0, 1), slice(9, 10))}
    for offset in range(TAPS):
        sx, sy, sz = offset // 9 - 1, offset // 3 % 3 - 1, offset % 3 - 1
        n = ids[brick * TAPS + offset]
        low = 8 + 8 * sz
        pad[span[sx][1], span[sy][1], low : low + 8, :] = look[n, span[sx][0], span[sy][0], :, :]
    for b in range(3):
        for c in range(3):
            window = pad[:, b : b + 8, 7 + c : 15 + c, :].reshape(640, LANES).astype(jnp.bfloat16)
            for a in range(3):
                k = 9 * a + 3 * b + c
                k = TAPS - 1 - k if flip else k
                col[:, k * LANES : (k + 1) * LANES] = window[a * 64 : a * 64 + VOX]


def mm(a, b, da=1, db=0):
    return lax.dot_general(a, b, (((da,), (db,)), ((), ())), preferred_element_type=jnp.float32)


def forward_kernel(ids, look, live, w, wd, order, pre_ref, strided_ref, piece_ref, pad, col):
    brick = pl.program_id(0)
    fill_columns(ids, look, pad, col, brick, False)
    pre = mm(col[...], w[...]) * live[0]
    pre_ref[0] = pre
    hidden = (pre * jax.nn.sigmoid(pre)).astype(jnp.bfloat16)
    strided = mm(order[...], hidden).astype(jnp.bfloat16)
    strided_ref[0] = strided
    total = None
    for t in range(8):
        term = mm(wd[t], strided[t * 64 : (t + 1) * 64], 1, 1)
        total = term if total is None else total + term
    piece_ref[0] = total.astype(jnp.bfloat16)


def weight_kernel(ids, look, live, gp, pre, strided, wd, order, gpre_ref, sub_ref, down_ref, pad, col):
    brick = pl.program_id(0)

    @pl.when(brick == 0)
    def _():
        sub_ref[...] = jnp.zeros_like(sub_ref)
        down_ref[...] = jnp.zeros_like(down_ref)

    fill_columns(ids, look, pad, col, brick, False)
    piece = gp[0]
    terms = []
    for t in range(8):
        down_ref[t] += mm(piece, strided[0, t * 64 : (t + 1) * 64])
        terms.append(mm(piece, wd[t], 0, 0))
    split = jnp.concatenate(terms, axis=0)
    high = split.astype(jnp.bfloat16)
    rest = (split - high.astype(jnp.float32)).astype(jnp.bfloat16)
    hidden = mm(order[...], high, 0, 0) + mm(order[...], rest, 0, 0)
    grad = (hidden * silu_slope(pre[0]) * live[0]).astype(jnp.bfloat16)
    gpre_ref[0] = grad
    sub_ref[...] += mm(grad, col[...], 0, 0)


def feature_kernel(ids, look, live, w, out_ref, pad, col):
    brick = pl.program_id(0)
    fill_columns(ids, look, pad, col, brick, True)
    out_ref[0] = (mm(col[...], w[...]) * live[0]).astype(jnp.bfloat16)


def whole(shape):
    return pl.BlockSpec(shape, lambda b, ids: (0,) * len(shape), pipeline_mode=pl.Buffered(1))


def summed(shape):
    return pl.BlockSpec(shape, lambda b, ids: (0,) * len(shape))


def each(shape):
    return pl.BlockSpec((1,) + shape, lambda b, ids: (b,) + (0,) * len(shape))


def call(kernel, bricks, in_specs, out_specs, out_shape, flops):
    return pl.pallas_call(
        kernel,
        grid_spec=pltpu.PrefetchScalarGridSpec(
            num_scalar_prefetch=1,
            grid=(bricks,),
            in_specs=in_specs,
            out_specs=out_specs,
            scratch_shapes=[
                pltpu.VMEM((10, 10, 24, LANES), jnp.float32),
                pltpu.VMEM((VOX, TAPS * LANES), jnp.bfloat16),
            ],
        ),
        out_shape=out_shape,
        compiler_params=pltpu.CompilerParams(
            dimension_semantics=("arbitrary",), vmem_limit_bytes=VMEM_BYTES
        ),
        cost_estimate=pl.CostEstimate(flops=flops, bytes_accessed=40_000_000, transcendentals=0),
    )


def rim_lookup(own, pick):
    bricks, voxels, channels = own.shape
    x = jnp.einsum("eb,bvc->evc", pick, own, preferred_element_type=jnp.float32)
    x = x.astype(jnp.bfloat16)[None, None]
    for axis, dim in (("gx", 0), ("yz", 1)):
        size = lax.axis_size(axis)
        up = [(i, (i + 1) % size) for i in range(size - 1)]
        down = [(j, i) for i, j in up]
        before = lax.ppermute(x, axis, up)
        after = lax.ppermute(x, axis, down)
        x = jnp.concatenate([before, x, after], axis=dim)
    arrived = x.reshape(-1, voxels, channels)
    everything = jnp.concatenate([own, arrived], axis=0)
    everything = jnp.pad(everything, ((0, 1), (0, 0), (0, LANES - channels)))
    return everything.astype(jnp.float32).reshape(-1, EDGE, EDGE, EDGE, LANES)


def on_device(
    features, occupancy, neighbours, exports, coarse_map, owners, w_sub, w_down, cotangent
):
    bricks, channels, voxels = features.shape
    coarse_channels = w_down.shape[1]
    groups = lax.axis_size("yz")
    f32, bf16 = jnp.float32, jnp.bfloat16
    ids = neighbours.reshape(-1)
    live = occupancy.astype(f32)[:, :, None]
    pick = (exports[:, None] == jnp.arange(bricks)[None, :]).astype(bf16)
    own = (features * occupancy.astype(bf16)[:, None, :]).transpose(0, 2, 1)
    look = rim_lookup(own, pick)

    lanes_more = LANES - channels
    w_in = jnp.pad(w_sub.transpose(0, 2, 1), ((0, 0), (0, lanes_more), (0, 0))).reshape(-1, channels)
    w_out = jnp.pad(w_sub, ((0, 0), (0, lanes_more), (0, 0))).reshape(-1, channels)
    order = jnp.asarray(fine_order(), bf16)

    cell = coarse_map[:, 0]
    earlier = jnp.arange(bricks)[None, :] < jnp.arange(bricks)[:, None]
    rank = jnp.sum((cell[:, None] == cell[None, :]) & earlier, axis=1)
    owner = jnp.sum(jnp.where(cell[:, None] == jnp.arange(owners.shape[0])[None, :], owners[None, :], 0), axis=1)
    select = (
        (owner[None, None, :] == jnp.arange(groups)[:, None, None])
        & (rank[None, None, :] == jnp.arange(3)[None, :, None])
    ).astype(bf16)
    octant = (coarse_map[:, 1][:, None] == jnp.arange(8)[None, :]).astype(bf16)
    place = jnp.einsum("grb,bp->grp", select, octant, preferred_element_type=f32).astype(bf16)
    place = lax.all_to_all(place, "yz", split_axis=0, concat_axis=0, tiled=True)
    spread = jnp.einsum(
        "srp,puv->sruv", place, jnp.asarray(block_order(), bf16), preferred_element_type=f32
    ).astype(bf16)
    cot_piece = jnp.einsum("scv,sruv->srcu", cotangent, spread, preferred_element_type=f32)

    conv_flops = 2 * bricks * VOX * TAPS * LANES * channels
    look_shape = look.shape
    pre, strided, piece = call(
        forward_kernel,
        bricks,
        [
            whole(look_shape),
            each((voxels, 1)),
            whole(w_in.shape),
            whole(w_down.shape),
            whole(order.shape),
        ],
        [each((voxels, channels)), each((voxels, channels)), each((coarse_channels, 64))],
        [
            jax.ShapeDtypeStruct((bricks, voxels, channels), f32),
            jax.ShapeDtypeStruct((bricks, voxels, channels), bf16),
            jax.ShapeDtypeStruct((bricks, coarse_channels, 64), bf16),
        ],
        conv_flops,
    )(ids, look, live, w_in, w_down, order)

    outgoing = jnp.einsum("grb,bcu->grcu", select, piece, preferred_element_type=f32).astype(bf16)
    arrived = lax.all_to_all(outgoing, "yz", split_axis=0, concat_axis=0, tiled=True)
    slope = silu_slope(arrived.astype(f32))
    back = (cot_piece * slope).astype(bf16)
    returned = lax.all_to_all(back, "yz", split_axis=0, concat_axis=0, tiled=True)
    coarse_pre = jnp.einsum("srcu,sruv->scv", arrived, spread, preferred_element_type=f32)
    coarse = jax.nn.silu(coarse_pre).astype(bf16)
    grad_piece = jnp.einsum("grb,grcu->bcu", select, returned, preferred_element_type=f32).astype(bf16)

    grad_pre, sub_local, down_local = call(
        weight_kernel,
        bricks,
        [
            whole(look_shape),
            each((voxels, 1)),
            each((coarse_channels, 64)),
            each((voxels, channels)),
            each((voxels, channels)),
            whole(w_down.shape),
            whole(order.shape),
        ],
        [
            each((voxels, channels)),
            summed((channels, TAPS * LANES)),
            summed(w_down.shape),
        ],
        [
            jax.ShapeDtypeStruct((bricks, voxels, channels), bf16),
            jax.ShapeDtypeStruct((channels, TAPS * LANES), f32),
            jax.ShapeDtypeStruct(w_down.shape, f32),
        ],
        conv_flops,
    )(ids, look, live, grad_piece, pre, strided, w_down, order)

    sub_local = sub_local.reshape(channels, TAPS, LANES)[:, :, :channels].transpose(1, 0, 2)
    grad_sub, grad_down = lax.psum((sub_local, down_local), ("gx", "yz"))

    grad_look = rim_lookup(grad_pre, pick)
    grad_own = call(
        feature_kernel,
        bricks,
        [whole(look_shape), each((voxels, 1)), whole(w_out.shape)],
        each((voxels, channels)),
        jax.ShapeDtypeStruct((bricks, voxels, channels), bf16),
        conv_flops,
    )(ids, grad_look, live, w_out)
    return (coarse, grad_own.transpose(0, 2, 1), grad_sub, grad_down)


def solution(mesh):
    split = ("gx", "yz")
    in_specs = (
        P(split, None, None),
        P(split, None),
        P(split, None),
        P(split),
        P(split, None),
        P(split),
        P(),
        P(),
        P(split, None, None),
    )
    out_specs = (P(split, None, None), P(split, None, None), P(), P())
    return jax.shard_map(
        on_device, mesh=mesh, in_specs=in_specs, out_specs=out_specs, check_vma=False
    )
```

```python
import jax
import jax.numpy as jnp
import numpy as np
from jax import lax
from jax.experimental import pallas as pl
from jax.experimental.pallas import tpu as pltpu
from jax.sharding import PartitionSpec as P

EDGE = 8
VOX = 512
LANES = 128
TAPS = 27
VMEM_BYTES = 56 * 2**20


def silu_slope(values):
    sig = jax.nn.sigmoid(values)
    return sig * (1.0 + values * (1.0 - sig))


def fine_order():
    ids = np.arange(VOX).reshape(4, 2, 4, 2, 4, 2).transpose(1, 3, 5, 0, 2, 4).reshape(-1)
    return np.eye(VOX, dtype=np.float32)[ids]


def block_order():
    ids = np.arange(VOX).reshape(2, 4, 2, 4, 2, 4).transpose(0, 2, 4, 1, 3, 5).reshape(-1)
    return np.eye(VOX, dtype=np.float32)[ids].reshape(8, 64, VOX)


def widen(own, arrived, look):
    bricks, channels = own.shape[0], own.shape[2]

    @pl.when(pl.program_id(0) == 0)
    def _():
        def put(source, first):
            def body(n, carry):
                block = source[n].astype(jnp.float32)
                rest = jnp.zeros((block.shape[0], LANES - channels), jnp.float32)
                look[first + n] = jnp.concatenate([block, rest], axis=1).reshape(EDGE, EDGE, EDGE, LANES)
                return carry

            lax.fori_loop(0, source.shape[0], body, 0)

        put(own, 0)
        put(arrived, bricks)
        last = bricks + arrived.shape[0]
        look[last] = jnp.zeros((EDGE, EDGE, EDGE, LANES), jnp.float32)


def fill_columns(ids, look, pad, col, brick, flip):
    span = {-1: (slice(7, 8), slice(0, 1)), 0: (slice(0, 8), slice(1, 9)), 1: (slice(0, 1), slice(9, 10))}
    for offset in range(TAPS):
        sx, sy, sz = offset // 9 - 1, offset // 3 % 3 - 1, offset % 3 - 1
        n = ids[brick * TAPS + offset]
        low = 8 + 8 * sz
        pad[span[sx][1], span[sy][1], low : low + 8, :] = look[n, span[sx][0], span[sy][0], :, :]
    for b in range(3):
        for c in range(3):
            window = pad[:, b : b + 8, 7 + c : 15 + c, :].reshape(640, LANES).astype(jnp.bfloat16)
            for a in range(3):
                k = 9 * a + 3 * b + c
                k = TAPS - 1 - k if flip else k
                col[:, k * LANES : (k + 1) * LANES] = window[a * 64 : a * 64 + VOX]


def mm(a, b, da=1, db=0):
    return lax.dot_general(a, b, (((da,), (db,)), ((), ())), preferred_element_type=jnp.float32)


def forward_kernel(ids, own, arrived, live, w, wd, order, pre_ref, strided_ref, piece_ref, look, pad, col):
    brick = pl.program_id(0)
    widen(own, arrived, look)
    fill_columns(ids, look, pad, col, brick, False)
    pre = mm(col[...], w[...]) * live[0]
    pre_ref[0] = pre
    hidden = (pre * jax.nn.sigmoid(pre)).astype(jnp.bfloat16)
    strided = mm(order[...], hidden).astype(jnp.bfloat16)
    strided_ref[0] = strided
    total = None
    for t in range(8):
        term = mm(wd[t], strided[t * 64 : (t + 1) * 64], 1, 1)
        total = term if total is None else total + term
    piece_ref[0] = total.astype(jnp.bfloat16)


def weight_kernel(ids, own, arrived, live, gp, pre, strided, wd, order, gpre_ref, sub_ref, down_ref, look, pad, col):
    brick = pl.program_id(0)

    @pl.when(brick == 0)
    def _():
        sub_ref[...] = jnp.zeros_like(sub_ref)
        down_ref[...] = jnp.zeros_like(down_ref)

    widen(own, arrived, look)
    fill_columns(ids, look, pad, col, brick, False)
    piece = gp[0]
    terms = []
    for t in range(8):
        down_ref[t] += mm(piece, strided[0, t * 64 : (t + 1) * 64])
        terms.append(mm(piece, wd[t], 0, 0))
    split = jnp.concatenate(terms, axis=0)
    high = split.astype(jnp.bfloat16)
    rest = (split - high.astype(jnp.float32)).astype(jnp.bfloat16)
    hidden = mm(order[...], high, 0, 0) + mm(order[...], rest, 0, 0)
    grad = (hidden * silu_slope(pre[0]) * live[0]).astype(jnp.bfloat16)
    gpre_ref[0] = grad
    sub_ref[...] += mm(grad, col[...], 0, 0)


def feature_kernel(ids, own, arrived, live, w, out_ref, look, pad, col):
    brick = pl.program_id(0)
    widen(own, arrived, look)
    fill_columns(ids, look, pad, col, brick, True)
    out_ref[0] = (mm(col[...], w[...]) * live[0]).astype(jnp.bfloat16)


def whole(shape):
    return pl.BlockSpec(shape, lambda b, ids: (0,) * len(shape), pipeline_mode=pl.Buffered(1))


def summed(shape):
    return pl.BlockSpec(shape, lambda b, ids: (0,) * len(shape))


def each(shape):
    return pl.BlockSpec((1,) + shape, lambda b, ids: (b,) + (0,) * len(shape))


def call(kernel, bricks, held, in_specs, out_specs, out_shape, flops):
    return pl.pallas_call(
        kernel,
        grid_spec=pltpu.PrefetchScalarGridSpec(
            num_scalar_prefetch=1,
            grid=(bricks,),
            in_specs=in_specs,
            out_specs=out_specs,
            scratch_shapes=[
                pltpu.VMEM((held, EDGE, EDGE, EDGE, LANES), jnp.float32),
                pltpu.VMEM((10, 10, 24, LANES), jnp.float32),
                pltpu.VMEM((VOX, TAPS * LANES), jnp.bfloat16),
            ],
        ),
        out_shape=out_shape,
        compiler_params=pltpu.CompilerParams(
            dimension_semantics=("arbitrary",), vmem_limit_bytes=VMEM_BYTES
        ),
        cost_estimate=pl.CostEstimate(flops=flops, bytes_accessed=100_000_000, transcendentals=0),
    )


def rim_lookup(own, pick):
    bricks, voxels, channels = own.shape
    x = jnp.einsum("eb,bvc->evc", pick, own, preferred_element_type=jnp.float32)
    x = x.astype(jnp.bfloat16)[None, None]
    for axis, dim in (("gx", 0), ("yz", 1)):
        size = lax.axis_size(axis)
        up = [(i, (i + 1) % size) for i in range(size - 1)]
        down = [(j, i) for i, j in up]
        before = lax.ppermute(x, axis, up)
        after = lax.ppermute(x, axis, down)
        x = jnp.concatenate([before, x, after], axis=dim)
    return x.reshape(-1, voxels, channels)


def on_device(
    features, occupancy, neighbours, exports, coarse_map, owners, w_sub, w_down, cotangent
):
    bricks, channels, voxels = features.shape
    coarse_channels = w_down.shape[1]
    groups = lax.axis_size("yz")
    f32, bf16 = jnp.float32, jnp.bfloat16
    ids = neighbours.reshape(-1)
    live = occupancy.astype(f32)[:, :, None]
    pick = (exports[:, None] == jnp.arange(bricks)[None, :]).astype(bf16)
    own = (features * occupancy.astype(bf16)[:, None, :]).transpose(0, 2, 1)
    around = rim_lookup(own, pick)
    held = bricks + around.shape[0] + 1

    lanes_more = LANES - channels
    w_in = jnp.pad(w_sub.transpose(0, 2, 1), ((0, 0), (0, lanes_more), (0, 0))).reshape(-1, channels)
    w_out = jnp.pad(w_sub, ((0, 0), (0, lanes_more), (0, 0))).reshape(-1, channels)
    order = jnp.asarray(fine_order(), bf16)

    cell = coarse_map[:, 0]
    earlier = jnp.arange(bricks)[None, :] < jnp.arange(bricks)[:, None]
    rank = jnp.sum((cell[:, None] == cell[None, :]) & earlier, axis=1)
    owner = jnp.sum(jnp.where(cell[:, None] == jnp.arange(owners.shape[0])[None, :], owners[None, :], 0), axis=1)
    select = (
        (owner[None, None, :] == jnp.arange(groups)[:, None, None])
        & (rank[None, None, :] == jnp.arange(3)[None, :, None])
    ).astype(bf16)
    octant = (coarse_map[:, 1][:, None] == jnp.arange(8)[None, :]).astype(bf16)
    place = jnp.einsum("grb,bp->grp", select, octant, preferred_element_type=f32).astype(bf16)
    place = lax.all_to_all(place, "yz", split_axis=0, concat_axis=0, tiled=True)
    spread = jnp.einsum(
        "srp,puv->sruv", place, jnp.asarray(block_order(), bf16), preferred_element_type=f32
    ).astype(bf16)
    cot_piece = jnp.einsum("scv,sruv->srcu", cotangent, spread, preferred_element_type=f32)

    conv_flops = 2 * bricks * VOX * TAPS * LANES * channels
    pre, strided, piece = call(
        forward_kernel,
        bricks,
        held,
        [
            whole(own.shape), whole(around.shape),
            each((voxels, 1)),
            whole(w_in.shape),
            whole(w_down.shape),
            whole(order.shape),
        ],
        [each((voxels, channels)), each((voxels, channels)), each((coarse_channels, 64))],
        [
            jax.ShapeDtypeStruct((bricks, voxels, channels), f32),
            jax.ShapeDtypeStruct((bricks, voxels, channels), bf16),
            jax.ShapeDtypeStruct((bricks, coarse_channels, 64), bf16),
        ],
        conv_flops,
    )(ids, own, around, live, w_in, w_down, order)

    outgoing = jnp.einsum("grb,bcu->grcu", select, piece, preferred_element_type=f32).astype(bf16)
    arrived = lax.all_to_all(outgoing, "yz", split_axis=0, concat_axis=0, tiled=True)
    slope = silu_slope(arrived.astype(f32))
    back = (cot_piece * slope).astype(bf16)
    returned = lax.all_to_all(back, "yz", split_axis=0, concat_axis=0, tiled=True)
    coarse_pre = jnp.einsum("srcu,sruv->scv", arrived, spread, preferred_element_type=f32)
    coarse = jax.nn.silu(coarse_pre).astype(bf16)
    grad_piece = jnp.einsum("grb,grcu->bcu", select, returned, preferred_element_type=f32).astype(bf16)

    grad_pre, sub_local, down_local = call(
        weight_kernel,
        bricks,
        held,
        [
            whole(own.shape), whole(around.shape),
            each((voxels, 1)),
            each((coarse_channels, 64)),
            each((voxels, channels)),
            each((voxels, channels)),
            whole(w_down.shape),
            whole(order.shape),
        ],
        [
            each((voxels, channels)),
            summed((channels, TAPS * LANES)),
            summed(w_down.shape),
        ],
        [
            jax.ShapeDtypeStruct((bricks, voxels, channels), bf16),
            jax.ShapeDtypeStruct((channels, TAPS * LANES), f32),
            jax.ShapeDtypeStruct(w_down.shape, f32),
        ],
        conv_flops,
    )(ids, own, around, live, grad_piece, pre, strided, w_down, order)

    sub_local = sub_local.reshape(channels, TAPS, LANES)[:, :, :channels].transpose(1, 0, 2)
    grad_sub, grad_down = lax.psum((sub_local, down_local), ("gx", "yz"))

    grad_around = rim_lookup(grad_pre, pick)
    grad_own = call(
        feature_kernel,
        bricks,
        held,
        [whole(own.shape), whole(around.shape), each((voxels, 1)), whole(w_out.shape)],
        each((voxels, channels)),
        jax.ShapeDtypeStruct((bricks, voxels, channels), bf16),
        conv_flops,
    )(ids, grad_pre, grad_around, live, w_out)
    return (coarse, grad_own.transpose(0, 2, 1), grad_sub, grad_down)


def solution(mesh):
    split = ("gx", "yz")
    in_specs = (
        P(split, None, None),
        P(split, None),
        P(split, None),
        P(split),
        P(split, None),
        P(split),
        P(),
        P(),
        P(split, None, None),
    )
    out_specs = (P(split, None, None), P(split, None, None), P(), P())
    return jax.shard_map(
        on_device, mesh=mesh, in_specs=in_specs, out_specs=out_specs, check_vma=False
    )
```
